128 devices in a mesh: band: 4 (over x), plane: 32 (over z, y, core).
Axes of the slice: x: 4, y: 4, z: 4, core: 2. Of those that a mesh axis runs over, the one named last changes fastest.
Arguments:
- orbitals: bfloat16 [2, 128, 13312, 128], P(None, 'band', 'plane')
- trial_bands: float32 [2, 4, 13312, 128], P(None, 'band', 'plane')
- potential: float32 [320, 320, 320], P('plane'), may hold values from -6 to 6
- stick_column: int32 [13312], P('plane'), may hold values from 0 to 16383, as said below
- stick_length: int32 [13312], P('plane'), may hold values from 0 to 127, as said below
Outputs:
- applied: float32 [2, 4, 13312, 128], P(None, 'band', 'plane')
- intersection: float32 [2, 128, 128], P(None, 'band')
- projected: float32 [2, 128, 4], P(None, 'band')
The draws below stay inside these ranges and needn't reach their ends.
Inputs may be any that keep to these rules, and one draw needn't show every extreme that they name: stick_column holds distinct window positions; every position x * 128 + y with (x - 64)^2 + (y - 64)^2 <= 63^2 appears once, and so do positions 0 and 16383; the remaining sticks take other positions. stick_length is 2 m + 1 for the largest whole m with m^2 + ox^2 + oy^2 <= 63^2 for the stick's column offsets ox, oy, and 0 where the column lies outside that disk.
All inputs are finite; a program needn't handle non-finite values.
Results may differ from the reference program's by a relative error of at most 0.0075.
Values may be sent and summed in bfloat16 or wider, within the bound.
A program may use at most 128 MiB of HBM per device.

```python
import jax
import jax.numpy as jnp
from jax import lax

GRID = 320
SLOT = 128
RADIUS = 63
STICKS = 13312
BANDS = 128
TRIALS = 4


shared_count = 4


def mixed_bands(key, band_count, salt):
    fields = jax.random.normal(key, (shared_count, 2, STICKS, SLOT), jnp.float32)
    key = jax.random.fold_in(key, salt)
    own_key, mix_key = jax.random.split(key)
    noises = jax.random.normal(own_key, (2, band_count, STICKS, SLOT), jnp.float32)
    weights = jax.random.normal(mix_key, (shared_count, band_count), jnp.float32) * 0.5
    mixture = noises
    for shared_index in range(shared_count):
        mixture = mixture + weights[shared_index][None, :, None, None] * fields[shared_index][:, None]
    return mixture * jnp.float32((2.0 / (STICKS * SLOT)) ** 0.5)


def sphere_sticks(key):
    centre = SLOT // 2
    places = jnp.arange(SLOT * SLOT, dtype=jnp.int32)
    off_x = places // SLOT - centre
    off_y = places % SLOT - centre
    radial = off_x * off_x + off_y * off_y
    within = (radial <= RADIUS * RADIUS).astype(jnp.int32)
    corners = ((places == 0) | (places == SLOT * SLOT - 1)).astype(jnp.int32)
    order_key, place_key = jax.random.split(key)
    ranked = jax.random.permutation(order_key, SLOT * SLOT).astype(jnp.int32)
    scores = within * (4 * SLOT * SLOT) + corners * (2 * SLOT * SLOT) + ranked
    chosen = lax.top_k(scores, STICKS)[1].astype(jnp.int32)
    chosen = jax.random.permutation(place_key, chosen).astype(jnp.int32)
    leeway = RADIUS * RADIUS - radial[chosen]
    steps_in = jnp.arange(1, SLOT // 2 + 1, dtype=jnp.int32)
    extent = jnp.sum((steps_in[None, :] * steps_in[None, :] <= leeway[:, None]).astype(jnp.int32), axis=1)
    length = jnp.where(leeway >= 0, 2 * extent + 1, 0).astype(jnp.int32)
    return (chosen, length)


def draw_orbitals(key, part):
    return mixed_bands(key, BANDS, 7).astype(jnp.bfloat16)


def draw_trial_bands(key, part):
    return mixed_bands(key, TRIALS, 11)


def draw_stick_column(key, part):
    chosen, length = sphere_sticks(key)
    return chosen


def draw_stick_length(key, part):
    chosen, length = sphere_sticks(key)
    return length


def levels(key, shape, cuts, smallest, largest):
    loudness = 1.0
    for dim, shards_of in cuts:
        steps = jax.random.uniform(jax.random.fold_in(jax.random.fold_in(key, 6), dim), (shards_of,), jnp.float32, smallest / len(cuts), largest / len(cuts))
        loudness = loudness * jnp.repeat(jnp.exp(steps), shape[dim] // shards_of).reshape((-1,) + (1,) * (len(shape) - 1 - dim))
    return loudness


def gaussian(key, dims, scale, most, pieces=(), kind=jnp.bfloat16):
    drawn = jax.random.normal(key, dims, jnp.float32) * scale
    if len(pieces) > 0:
        drawn = levels(key, dims, pieces, -0.22, 0.18) * drawn
    return jnp.clip(drawn, min=-most, max=most).astype(kind)


def setup_inputs(seed: int = 0) -> dict:
    key_list = jax.random.split(jax.random.key(seed), 6)
    orbitals = draw_orbitals(jax.random.fold_in(key_list[5], 71), 0)
    trial_bands = draw_trial_bands(jax.random.fold_in(key_list[5], 71), 0)
    potential = gaussian(key_list[2], (GRID, GRID, GRID), 1.0, 6.0, ((0, 32),), jnp.float32)
    stick_column = draw_stick_column(jax.random.fold_in(key_list[5], 71), 0)
    stick_length = draw_stick_length(jax.random.fold_in(key_list[5], 71), 0)
    return dict(orbitals=orbitals, trial_bands=trial_bands, potential=potential, stick_column=stick_column, stick_length=stick_length)


def sphere_masks(stick_column, stick_length):
    centre = SLOT // 2
    slot_offsets = jnp.arange(SLOT, dtype=jnp.int32) - centre
    inside = 2 * jnp.abs(slot_offsets)[None, :] < stick_length[:, None]
    off_x = stick_column // SLOT - centre
    off_y = stick_column % SLOT - centre
    squared = (off_x * off_x + off_y * off_y)[:, None] + (slot_offsets * slot_offsets)[None, :]
    kinetic = squared.astype(jnp.float32) / jnp.float32(RADIUS * RADIUS)
    return inside, kinetic, off_x, off_y, slot_offsets


def to_low(values):
    real_low, imag_low = lax.optimization_barrier((jnp.real(values).astype(jnp.bfloat16), jnp.imag(values).astype(jnp.bfloat16)))
    return lax.complex(real_low.astype(jnp.real(values).dtype), imag_low.astype(jnp.real(values).dtype))


def local_term(parts_in, potential, index_z, index_y, index_x):
    grid_shape = (GRID, GRID, GRID)
    real_grid = jnp.zeros(grid_shape, parts_in.dtype).at[index_z, index_y, index_x].set(parts_in[0])
    imag_grid = jnp.zeros(grid_shape, parts_in.dtype).at[index_z, index_y, index_x].set(parts_in[1])
    stick_waves = to_low(jnp.fft.ifft(lax.complex(real_grid, imag_grid), axis=0) * GRID)
    waves = jnp.fft.ifft2(stick_waves, axes=(1, 2)) * (GRID * GRID)
    plane_spectrum = to_low(jnp.fft.fft2(waves * potential, axes=(1, 2)) / (GRID * GRID))
    spectrum = jnp.fft.fft(plane_spectrum, axis=0) / GRID
    picked = spectrum[index_z, index_y, index_x]
    return jnp.stack([jnp.real(picked), jnp.imag(picked)])


def pair_products(left, right):
    rows_left = left.reshape(2, left.shape[1], -1)
    rows_right = right.reshape(2, right.shape[1], -1)

    def real_dot(first, second):
        return jnp.dot(first, second.T, preferred_element_type=jnp.float32)

    real_part = real_dot(rows_left[0], rows_right[0]) + real_dot(rows_left[1], rows_right[1])
    imag_part = real_dot(rows_left[0], rows_right[1]) - real_dot(rows_left[1], rows_right[0])
    return jnp.stack([real_part, imag_part])


def reference(orbitals, trial_bands, potential, stick_column, stick_length):
    inside, kinetic, off_x, off_y, slot_offsets = sphere_masks(stick_column, stick_length)
    masked = jnp.where(inside[None, None], trial_bands, jnp.zeros_like(trial_bands))
    basis = jnp.where(inside[None, None], orbitals, jnp.zeros_like(orbitals))
    index_z = (slot_offsets % GRID)[None, :]
    index_y = (off_y % GRID)[:, None]
    index_x = (off_x % GRID)[:, None]
    by_band = jnp.transpose(masked, (1, 0, 2, 3))
    local_part = lax.map(lambda parts_in: local_term(parts_in, potential, index_z, index_y, index_x), by_band)
    local_part = jnp.transpose(local_part, (1, 0, 2, 3))
    applied = jnp.where(inside[None, None], kinetic[None, None] * trial_bands + local_part, jnp.zeros_like(trial_bands))
    applied_low = applied.astype(jnp.bfloat16)
    intersection = pair_products(basis, basis)
    projected = pair_products(basis, applied_low)
    return (applied, intersection, projected)
```

```python
import functools
import math

import jax
import jax.numpy as jnp
import ml_dtypes
import numpy as np
from jax import lax
from jax.experimental import pallas as pl
from jax.experimental.pallas import tpu as pltpu
from jax.sharding import PartitionSpec as P

MESH = pl.DeviceIdType.MESH
BF16 = jnp.bfloat16
F32 = jnp.float32

GRID = 320
SLOT = 128
RADIUS = 63
NB = 4
NP = 32
SD = 416
ZP = GRID // NP
KZ = 2 * ZP
ROWS = 80
STICKS = NP * SD
PAD = 384
TILES = 6
EXTRA = 8 * SLOT
GROUP = 4 * SD
GROUPS = NP // 4
REDUCERS = 10


def split(table):
    table = np.asarray(table, np.float32)
    high = table.astype(ml_dtypes.bfloat16)
    low = (table - high.astype(np.float32)).astype(ml_dtypes.bfloat16)
    return high, low


@functools.lru_cache
def tables():
    half = SLOT // 2
    phase = np.outer(np.arange(SLOT) - half, np.arange(GRID)) % GRID
    cos, sin = np.cos(2 * math.pi / GRID * phase), np.sin(2 * math.pi / GRID * phase)
    full = np.zeros((NP, KZ, 2, SLOT))
    for q in range(NP):
        c, s = cos[:, q * ZP : (q + 1) * ZP].T, sin[:, q * ZP : (q + 1) * ZP].T
        full[q, :ZP, 0], full[q, :ZP, 1] = c, -s
        full[q, ZP:, 0], full[q, ZP:, 1] = s, c
    main = full[:, :16].reshape(NP * 16, 2 * SLOT)
    rest = np.tile(full[:, 16:], (1, 4, 1, 1)).reshape(NP * 16, 2 * SLOT)
    z_out = np.stack([*split(main), *split(rest)])
    z_back = np.stack([*split(main.T / GRID), *split(rest.T / GRID)])
    x_out = np.zeros((2, SLOT, 2, PAD))
    x_out[0, :, 0, :GRID], x_out[0, :, 1, :GRID] = cos, sin
    x_out[1, :, 0, :GRID], x_out[1, :, 1, :GRID] = -sin, cos
    x_out = x_out.reshape(2 * SLOT, 2 * PAD)
    y_out = np.block([[cos.T, -sin.T], [sin.T, cos.T]])
    low = ml_dtypes.bfloat16
    return dict(
        z_out=z_out,
        z_back=z_back,
        x_out=x_out.astype(low),
        y_out=y_out.astype(low),
        y_back=(y_out.T / GRID).astype(low),
        x_back=(x_out.T / GRID).astype(low),
        swap=np.eye(256).reshape(16, 16, 256).transpose(1, 0, 2).reshape(256, 256).astype(low),
    )


TABLES = ("z_out", "z_back", "x_out", "y_out", "y_back", "x_back", "swap")


def dot(first, second):
    return jnp.dot(first, second, preferred_element_type=F32)


def dot_nt(first, second):
    return lax.dot_general(first, second, (((1,), (1,)), ((), ())), preferred_element_type=F32)


def kernel(
    orbitals, trial, potential, meta, z_out_h, z_back_h, x_out_h, y_out_h, y_back_h, x_back_h, swap_h,
    applied_out, final_out,
    z_out, z_back, x_out, y_out, y_back, x_back, swap, pot,
    shares, masked, cols_out, cols_in, tx, rx, tx2, rx2,
    spots, values, onehot, spread, window, back,
    xin, yin, prod, xback, inside_s, inside_low, kinetic_s, local_s, applied, applied_low, applied_in,
    turned, turned_applied, extra_raw, extra_out, extra_in, gram, proj,
    part_out, part_in, part_sum, red_in, fin,
    load_sem, share_send, share_recv, own_sem, extra_send, extra_recv, cols_send, cols_recv, tx_send, tx_recv, tx2_send, tx2_recv,
    app_send, app_recv, part_send, part_recv, red_send, red_recv, fin_send, fin_recv, out_sem,
):
    b = lax.axis_index("band")
    p = lax.axis_index("plane")

    barrier = pltpu.get_barrier_semaphore()

    def plane_peer(i):
        return 4 * lax.rem(p // 4 + i // 4, GROUPS) + lax.rem(p + i, 4)

    def greet(i, carry):
        pl.semaphore_signal(barrier, inc=1, device_id=(b, plane_peer(i)), device_id_type=MESH)
        return carry

    lax.fori_loop(1, NP, greet, 0)
    for d in range(1, NB):
        pl.semaphore_signal(barrier, inc=1, device_id=(lax.rem(b + d, NB), p), device_id_type=MESH)

    loads = [
        pltpu.make_async_copy(source, target, load_sem.at[i])
        for i, (source, target) in enumerate(
            [
                (z_out_h, z_out), (z_back_h, z_back), (x_out_h, x_out), (y_out_h, y_out), (y_back_h, y_back),
                (x_back_h, x_back), (swap_h, swap), (potential, pot),
                (orbitals.at[:, :, pl.ds(16 * 4 * TILES, 32), :], extra_raw),
            ]
        )
    ]
    for load in loads:
        load.start()

    shift = 32 * lax.rem(p, 4)
    rest = 384 + pl.multiple_of(shift, 32)
    cols_out[0:3, :] = meta[0:3, :]
    cols_out[3:4, :] = pltpu.roll(meta[0:8, :], shift, 1)[3:4, :]
    cols_out[4:8, :] = jnp.zeros((4, SLOT), jnp.int32)
    slots = lax.broadcasted_iota(jnp.int32, (SLOT, SLOT), 1) - SLOT // 2
    for t in range(4):
        rows = SLOT if t < 3 else SD - 3 * SLOT
        as_column = jnp.broadcast_to(meta[t : t + 1, :].astype(F32), (SLOT, SLOT)).T.astype(jnp.int32)
        length = jnp.broadcast_to(meta[4 + t : 5 + t, :].astype(F32), (SLOT, SLOT)).T.astype(jnp.int32)
        inside = (2 * jnp.abs(slots) < length).astype(F32)
        off_x, off_y = (as_column >> 7) - SLOT // 2, (as_column & 127) - SLOT // 2
        squared = off_x * off_x + off_y * off_y + slots * slots
        kinetic = squared.astype(F32) / F32(RADIUS * RADIUS)
        where = pl.ds(t * SLOT, rows)
        inside_s[where, :] = inside[:rows]
        kinetic_s[where, :] = kinetic[:rows]
    inside_low[...] = inside_s[...].astype(BF16)

    for k in range(2):
        masked[k, 384:512, :] = jnp.zeros((SLOT, SLOT), F32)
        masked[k, 0:384, :] = trial[k, 0, 0:384, :] * inside_s[0:384, :]
        masked[k, pl.ds(rest, 32), :] = trial[k, 0, 384:SD, :] * inside_s[384:SD, :]
    turned_trial = jnp.concatenate([masked[0].T, masked[1].T], axis=0)
    high = turned_trial.astype(BF16)
    low = (turned_trial - high.astype(F32)).astype(BF16)
    loads[0].wait()

    def z_dot(i):
        return dot(z_out[i], high) + (dot(z_out[i + 1], high) + dot(z_out[i], low))

    main = z_dot(0)
    for t in range(4):
        tx[:, 16 * t : 16 * t + 16, :] = main[:, t * SLOT : (t + 1) * SLOT].reshape(NP, 16, SLOT).astype(BF16)
    every = z_dot(2)
    quarter = (lax.broadcasted_iota(jnp.int32, (NP * 16, SLOT), 0) >> 2) & 3
    tail = jnp.zeros((NP * 16, SLOT), F32)
    for t in range(4):
        tail = jnp.where(quarter == t, every[:, t * SLOT : (t + 1) * SLOT], tail)
    tx[:, 64:80, :] = tail.reshape(NP, 16, SLOT).astype(BF16)

    def block_copy(q, source, out_ref, in_ref, send, recv):
        return pltpu.make_async_remote_copy(
            src_ref=out_ref.at[q], dst_ref=in_ref.at[source], send_sem=send, recv_sem=recv,
            device_id=(b, q), device_id_type=MESH,
        )

    def all_copies(out_ref, in_ref, send, recv, first=0, count=NP - 1):
        where = pl.ds(first, count)
        return pltpu.make_async_remote_copy(
            src_ref=out_ref.at[where], dst_ref=in_ref.at[where], send_sem=send, recv_sem=recv,
            device_id=(b, lax.rem(p + 1, NP)), device_id_type=MESH,
        )

    pl.semaphore_wait(barrier, NP - 1 + NB - 1)

    def share_rows(c, j):
        return pl.ds(pl.multiple_of((TILES * c + j) * 16, 16), 16)

    def share_copy(c, j, source):
        return pltpu.make_async_remote_copy(
            src_ref=orbitals.at[:, :, share_rows(c, j), :], dst_ref=shares.at[source, j],
            send_sem=share_send.at[c, j], recv_sem=share_recv.at[source, j],
            device_id=(c, p), device_id_type=MESH,
        )

    def own_copy(j):
        return pltpu.make_async_copy(orbitals.at[:, :, share_rows(b, j), :], shares.at[b, j], own_sem.at[j])

    def send_shares(j, carry):
        for d in range(1, NB):
            share_copy(lax.rem(b + d, NB), j, b).start()
        own_copy(j).start()
        return carry

    send_shares(0, 0)

    def cols_copy(q, source):
        return pltpu.make_async_remote_copy(
            src_ref=cols_out, dst_ref=cols_in.at[source], send_sem=cols_send, recv_sem=cols_recv,
            device_id=(b, q), device_id_type=MESH,
        )

    def send_cols(i, carry):
        cols_copy(plane_peer(i), p).start()
        return carry

    lax.fori_loop(1, NP, send_cols, 0)

    def send_tx(i, carry):
        block_copy(plane_peer(i), p, tx, rx, tx_send, tx_recv.at[p // 4]).start()
        return carry

    lax.fori_loop(1, NP, send_tx, 0)
    cols_in[p] = cols_out[...]
    rx[p] = tx[p]

    lax.fori_loop(1, TILES, send_shares, 0)

    gram[...] = jnp.zeros_like(gram)
    proj[...] = jnp.zeros_like(proj)

    def gram_step(j):
        own_copy(j).wait()
        for d in range(1, NB):
            c = lax.rem(b + d, NB)
            share_copy(c, j, c).wait_recv()
        mask = inside_low[share_rows(b, j), :]
        for k in range(2):
            for c in range(NB):
                halves = [
                    (shares[c, j, k, half * 16 : (half + 1) * 16] * mask[None]).reshape(256, SLOT) for half in range(2)
                ]
                flipped = dot(swap[...], jnp.concatenate(halves, axis=1)).astype(BF16)
                for half in range(2):
                    row = k * 128 + c * 32 + half * 16
                    for i in range(16):
                        lane = j * 2048 + i * SLOT
                        turned[row : row + 16, lane : lane + SLOT] = flipped[
                            i * 16 : i * 16 + 16, half * SLOT : (half + 1) * SLOT
                        ]
        block = turned[:, j * 2048 : (j + 1) * 2048]
        gram[...] += dot_nt(block, block)

    all_copies(cols_in, cols_in, cols_send, cols_recv).wait_recv()

    def group_lanes(g):
        return pl.ds(pl.multiple_of(g * GROUP, SLOT), GROUP)

    def fill_onehot(g, carry):
        where = group_lanes(g)
        pieces = [cols_in[4 * g + r, t : t + 1, :] for r in range(4) for t in range(3)]
        pieces.append(sum(cols_in[4 * g + r, 3:4, :] for r in range(1, 4)) + cols_in[4 * g, 3:4, :])
        group_cols = jnp.concatenate(pieces, axis=1)
        col_y = group_cols & 127
        spot = ((col_y >> 5) << 7) + (group_cols >> 7)
        spots[0:1, where] = col_y & 31
        for r in range(4):
            ids = lax.broadcasted_iota(jnp.int32, (SLOT, GROUP), 0) + r * SLOT
            onehot[r * SLOT : (r + 1) * SLOT, where] = (ids == spot).astype(F32).astype(BF16)
        return carry

    lax.fori_loop(0, GROUPS, fill_onehot, 0)

    window[...] = jnp.zeros_like(window)

    def to_window(i, carry):
        g = lax.rem(p // 4 + GROUPS - i, GROUPS)
        where = group_lanes(g)

        @pl.when(i == 0)
        def _():
            all_copies(tx, rx, tx_send, tx_recv.at[g], 0, 3).wait_recv()

        @pl.when(i > 0)
        def _():
            all_copies(tx, rx, tx_send, tx_recv.at[g], 0, 4).wait_recv()

        rest_block = jnp.zeros((32, SLOT), F32)
        for r in range(4):
            block = rx[4 * g + r].astype(F32)
            for t in range(3):
                lane = (3 * r + t) * SLOT
                values[0:16, lane : lane + SLOT] = block[16 * t : 16 * t + 16]
                values[16:20, lane : lane + SLOT] = block[64 + 4 * t : 68 + 4 * t]
            rest_block = rest_block + block[48:80]
        values[0:16, 12 * SLOT : GROUP] = rest_block[0:16]
        values[16:20, 12 * SLOT : GROUP] = rest_block[28:32]
        here = lax.broadcasted_iota(jnp.int32, (32, GROUP), 0) == spots[0:1, where]
        for r in range(KZ):
            spread[r * 32 : (r + 1) * 32, :] = jnp.where(here, values[r : r + 1, :], 0.0).astype(BF16)
        window[...] += dot_nt(spread[...], onehot[:, where])
        return carry

    lax.fori_loop(0, GROUPS, to_window, 0)

    loads[6].wait()
    loads[8].wait()
    for t in range(2):
        mask = inside_low[384 + 16 * t : 400 + 16 * t, :]
        for k in range(2):
            halves = [
                (extra_raw[k, half * 16 : (half + 1) * 16, 16 * t : 16 * t + 16] * mask[None]).reshape(256, SLOT)
                for half in range(2)
            ]
            flipped = dot(swap[...], jnp.concatenate(halves, axis=1)).astype(BF16)
            for half in range(2):
                for i in range(16):
                    lane = (16 * t + i) * SLOT
                    extra_out[k, half * 16 : half * 16 + 16, lane : lane + SLOT] = flipped[
                        i * 16 : i * 16 + 16, half * SLOT : (half + 1) * SLOT
                    ]

    def extra_copy(c, source):
        return pltpu.make_async_remote_copy(
            src_ref=extra_out.at[:, :, pl.ds(pl.multiple_of(c * EXTRA, EXTRA), EXTRA)], dst_ref=extra_in.at[source],
            send_sem=extra_send.at[c], recv_sem=extra_recv.at[source], device_id=(c, p), device_id_type=MESH,
        )

    gram_step(0)

    for load in loads[2:6]:
        load.wait()
    loads[7].wait()
    prod[...] = jnp.zeros_like(prod)

    def planes(i, carry):
        for h in range(2):
            z = 2 * i + h
            for k in range(2):
                for v in range(4):
                    piece = window[pl.ds(pl.multiple_of((k * ZP + z) * 32, 32), 32), v * SLOT : (v + 1) * SLOT]
                    rows = h * SLOT + v * 32
                    xin[rows : rows + 32, k * SLOT : (k + 1) * SLOT] = piece.astype(BF16)
        along_x = dot(xin[...], x_out[...])
        for h in range(2):
            for k in range(2):
                piece = along_x[h * SLOT : (h + 1) * SLOT, k * PAD : (k + 1) * PAD]
                yin[k * SLOT : (k + 1) * SLOT, h * PAD : (h + 1) * PAD] = piece.astype(BF16)
        spatial = dot(y_out[...], yin[...])
        for h in range(2):
            field = pot[2 * i + h]
            for k in range(2):
                piece = spatial[k * GRID : (k + 1) * GRID, h * PAD : h * PAD + GRID]
                prod[k * GRID : (k + 1) * GRID, h * PAD : h * PAD + GRID] = (piece * field).astype(BF16)
        back_y = dot(y_back[...], prod[...])
        for h in range(2):
            for k in range(2):
                piece = back_y[k * SLOT : (k + 1) * SLOT, h * PAD : (h + 1) * PAD]
                xback[h * SLOT : (h + 1) * SLOT, k * PAD : (k + 1) * PAD] = piece.astype(BF16)
        back_x = dot(xback[...], x_back[...])
        for h in range(2):
            z = 2 * i + h
            for k in range(2):
                for v in range(4):
                    rows = h * SLOT + v * 32
                    piece = back_x[rows : rows + 32, k * SLOT : (k + 1) * SLOT]
                    where = pl.ds(pl.multiple_of((k * ZP + z) * 32, 32), 32)
                    back[where, v * SLOT : (v + 1) * SLOT] = piece.astype(BF16)
        return carry

    lax.fori_loop(0, ZP // 2, planes, 0)

    gram_step(1)

    def from_window(i, carry):
        g = lax.rem(p // 4 + 1 + i, GROUPS)
        where = group_lanes(g)
        here = lax.broadcasted_iota(jnp.int32, (32, GROUP), 0) == spots[0:1, where]
        found = dot(back[...], onehot[:, where])
        for r in range(KZ):
            picked = jnp.where(here, found[r * 32 : (r + 1) * 32], 0.0)
            values[r : r + 1, :] = jnp.sum(picked, axis=0, keepdims=True)
        for r in range(4):
            q = 4 * g + r
            lanes = [slice((3 * r + t) * SLOT, (3 * r + t + 1) * SLOT) for t in range(3)] + [slice(12 * SLOT, GROUP)]
            for t in range(4):
                tx2[q, 16 * t : 16 * t + 16, :] = values[0:16, lanes[t]].astype(BF16)
            tx2[q, 64:80, :] = jnp.concatenate([values[16:20, lane] for lane in lanes], axis=0).astype(BF16)

        def send_back(r, carry):
            q = 4 * g + r

            @pl.when(q != p)
            def _():
                block_copy(q, p, tx2, rx2, tx2_send, tx2_recv).start()

            return carry

        lax.fori_loop(0, 4, send_back, 0)
        return carry

    lax.fori_loop(0, GROUPS, from_window, 0)
    rx2[p] = tx2[p]
    gram_step(2)

    all_copies(tx2, rx2, tx2_send, tx2_recv).wait_recv()

    loads[1].wait()
    rest_low = rx2[:, 64:80, :].reshape(NP * 16, SLOT).astype(F32)
    for t in range(4):
        first = rx2[:, 16 * t : 16 * t + 16, :].reshape(NP * 16, SLOT)
        second = jnp.where(quarter == t, rest_low, 0.0).astype(BF16)
        turned_local = (dot(z_back[0], first) + dot(z_back[2], second)) + (
            dot(z_back[1], first) + dot(z_back[3], second)
        )
        for k in range(2):
            local_s[k, t * SLOT : (t + 1) * SLOT, :] = turned_local[k * SLOT : (k + 1) * SLOT].T
    for k in range(2):
        for where, source in ((slice(0, 384), slice(0, 384)), (slice(384, SD), pl.ds(rest, 32))):
            kept = inside_s[where, :] * (kinetic_s[where, :] * trial[k, 0, where, :] + local_s[k, source, :])
            applied[k, 0, where, :] = kept
            applied_low[k, where, :] = kept.astype(BF16)
    applied_write = pltpu.make_async_copy(applied, applied_out, out_sem)
    applied_write.start()

    def app_rows(c, j):
        if j < TILES:
            return share_rows(c, j)
        return pl.ds(pl.multiple_of((4 * TILES + c // 2) * 16, 16), 16)

    def app_copy(c, j, source):
        return pltpu.make_async_remote_copy(
            src_ref=applied_low.at[:, app_rows(c, j), :], dst_ref=applied_in.at[j, source],
            send_sem=app_send.at[c, j], recv_sem=app_recv.at[source, j],
            device_id=(c, p), device_id_type=MESH,
        )

    for j in range(TILES + 1):
        for d in range(1, NB):
            app_copy(lax.rem(b + d, NB), j, b).start()
        applied_in[j, b] = applied_low[:, app_rows(b, j), :]
    for d in range(1, NB):
        extra_copy(lax.rem(b + d, NB), b).start()
    extra_in[b] = extra_out[:, :, pl.ds(pl.multiple_of(b * EXTRA, EXTRA), EXTRA)]
    gram_step(3)
    gram_step(4)

    def applied_rows(j):
        for d in range(1, NB):
            c = lax.rem(b + d, NB)
            app_copy(c, j, c).wait_recv()
        empty = jnp.zeros((4, 16, SLOT), BF16)
        pieces = [applied_in[j, c, k][None] for k in range(2) for c in range(NB)]
        gathered = jnp.concatenate(pieces[:4] + [empty] + pieces[4:] + [empty], axis=0).reshape(256, SLOT)
        flipped = dot(swap[...], gathered).astype(BF16)
        for i in range(16):
            turned_applied[:, i * SLOT : (i + 1) * SLOT] = flipped[i * 16 : i * 16 + 16]

    def applied_step(j):
        applied_rows(j)
        proj[...] += dot_nt(turned_applied[...], turned[:, j * 2048 : (j + 1) * 2048])

    for j in range(5):
        applied_step(j)
    gram_step(5)
    applied_step(5)
    for d in range(1, NB):
        c = lax.rem(b + d, NB)
        extra_copy(c, c).wait_recv()
    extra = jnp.concatenate([extra_in[c, k] for k in range(2) for c in range(NB)], axis=0)
    gram[...] += dot_nt(extra, extra)
    applied_rows(TILES)
    half = pl.ds(pl.multiple_of(lax.rem(b, 2) * EXTRA, EXTRA), EXTRA)
    proj[...] += dot_nt(turned_applied[:, half], extra)

    real = gram[0:128, 0:128] + gram[128:256, 128:256]
    imag = gram[0:128, 128:256] - gram[128:256, 0:128]
    proj_real = proj[0:8, 0:128] + proj[8:16, 128:256]
    proj_imag = proj[8:16, 0:128] - proj[0:8, 128:256]
    for c in range(NB):
        part_out[c, 0:32, :] = real[c * 32 : (c + 1) * 32]
        part_out[c, 32:64, :] = imag[c * 32 : (c + 1) * 32]
        part_out[c, 64:72, :] = proj_real
        part_out[c, 72:80, :] = proj_imag

    def part_copy(c, source):
        return pltpu.make_async_remote_copy(
            src_ref=part_out.at[c], dst_ref=part_in.at[source], send_sem=part_send.at[c], recv_sem=part_recv.at[source],
            device_id=(c, p), device_id_type=MESH,
        )

    for d in range(1, NB):
        part_copy(lax.rem(b + d, NB), b).start()
    part_in[b] = part_out[b]
    for d in range(1, NB):
        c = lax.rem(b + d, NB)
        part_copy(c, c).wait_recv()
    part_sum[...] = ((part_in[0] + part_in[1]) + (part_in[2] + part_in[3])).reshape(REDUCERS, 8, SLOT)

    def red_copy(t):
        return pltpu.make_async_remote_copy(
            src_ref=part_sum.at[t], dst_ref=red_in.at[p], send_sem=red_send.at[t], recv_sem=red_recv,
            device_id=(b, 3 * t), device_id_type=MESH,
        )

    def fin_copy(t, q):
        return pltpu.make_async_remote_copy(
            src_ref=fin.at[t], dst_ref=fin.at[t], send_sem=fin_send, recv_sem=fin_recv.at[t],
            device_id=(b, q), device_id_type=MESH,
        )

    mine = p // 3
    reducer = jnp.logical_and(lax.rem(p, 3) == 0, mine < REDUCERS)

    def send_red(t, carry):
        @pl.when(3 * t != p)
        def _():
            red_copy(t).start()

        return carry

    lax.fori_loop(0, REDUCERS, send_red, 0)

    @pl.when(reducer)
    def _():
        red_in[p] = part_sum[mine]
        all_copies(red_in, red_in, fin_send, red_recv).wait_recv()
        fin[mine] = jnp.sum(red_in[...], axis=0)

        def send_fin(i, carry):
            fin_copy(mine, plane_peer(i)).start()
            return carry

        lax.fori_loop(1, NP, send_fin, 0)

    def wait_fin(t, carry):
        @pl.when(3 * t != p)
        def _():
            fin_copy(t, 3 * t).wait_recv()

        return carry

    lax.fori_loop(0, REDUCERS, wait_fin, 0)
    final_out[...] = fin[...]

    all_copies(cols_in, cols_in, cols_send, cols_recv).wait_send()
    all_copies(tx, rx, tx_send, tx_recv.at[0]).wait_send()
    all_copies(tx2, rx2, tx2_send, tx2_recv).wait_send()

    @pl.when(reducer)
    def _():
        all_copies(red_in, red_in, fin_send, red_recv).wait_send()

    def red_sent(t, carry):
        @pl.when(3 * t != p)
        def _():
            red_copy(t).wait_send()

        return carry

    lax.fori_loop(0, REDUCERS, red_sent, 0)
    for d in range(1, NB):
        c = lax.rem(b + d, NB)
        extra_copy(c, b).wait_send()
        part_copy(c, b).wait_send()
        for j in range(TILES):
            share_copy(c, j, b).wait_send()
        for j in range(TILES + 1):
            app_copy(c, j, b).wait_send()
    applied_write.wait()


def finish(applied, final, applied_out, intersection, projected):
    applied_out[...] = applied[...]
    shift = lax.rem(SLOT - lax.axis_index("band") * 32, SLOT)
    for k in range(2):
        for r in range(4):
            intersection[k, 8 * r : 8 * r + 8, :] = final[4 * k + r]
        projected[k] = pltpu.roll(final[8 + k], shift, 1)[0:NB, 0:32]


def shards(orbitals, trial_bands, potential, stick_column, stick_length):
    pad = (0, 4 * SLOT - SD)
    meta = jnp.concatenate([jnp.pad(stick_column, pad), jnp.pad(stick_length, pad)]).reshape(8, SLOT)
    held = tables()
    any_spec = pl.BlockSpec(memory_space=pl.ANY)
    vmem_spec = pl.BlockSpec(memory_space=pltpu.VMEM)
    vmem = pltpu.VMEM
    sem = pltpu.SemaphoreType.DMA
    applied, final = pl.pallas_call(
        kernel,
        out_shape=(
            jax.ShapeDtypeStruct(trial_bands.shape, F32),
            jax.ShapeDtypeStruct((REDUCERS, 8, SLOT), F32),
        ),
        in_specs=[any_spec, vmem_spec, any_spec, vmem_spec] + [any_spec] * len(TABLES),
        out_specs=(any_spec, vmem_spec),
        scratch_shapes=[vmem(held[name].shape, BF16) for name in TABLES]
        + [
            vmem((ZP, GRID, GRID), F32),
            vmem((NB, TILES, 2, 32, 16, SLOT), BF16),
            vmem((2, 512, SLOT), F32),
            vmem((8, SLOT), jnp.int32),
            vmem((NP, 8, SLOT), jnp.int32),
            vmem((NP, ROWS, SLOT), BF16),
            vmem((NP, ROWS, SLOT), BF16),
            vmem((NP, ROWS, SLOT), BF16),
            vmem((NP, ROWS, SLOT), BF16),
            vmem((8, STICKS), jnp.int32),
            vmem((24, GROUP), F32),
            vmem((4 * SLOT, STICKS), BF16),
            vmem((KZ * 32, GROUP), BF16),
            vmem((KZ * 32, 4 * SLOT), F32),
            vmem((KZ * 32, 4 * SLOT), BF16),
            vmem((2 * SLOT, 2 * SLOT), BF16),
            vmem((2 * SLOT, 2 * PAD), BF16),
            vmem((2 * GRID, 2 * PAD), BF16),
            vmem((2 * SLOT, 2 * PAD), BF16),
            vmem((SD, SLOT), F32),
            vmem((SD, SLOT), BF16),
            vmem((SD, SLOT), F32),
            vmem((2, 512, SLOT), F32),
            vmem((2, 1, SD, SLOT), F32),
            vmem((2, SD, SLOT), BF16),
            vmem((TILES + 1, NB, 2, 16, SLOT), BF16),
            vmem((256, TILES * 2048), BF16),
            vmem((16, 2048), BF16),
            vmem((2, 32, 32, SLOT), BF16),
            vmem((2, 32, 32 * SLOT), BF16),
            vmem((NB, 2, 32, EXTRA), BF16),
            vmem((256, 256), F32),
            vmem((16, 256), F32),
            vmem((NB, 80, SLOT), F32),
            vmem((NB, 80, SLOT), F32),
            vmem((REDUCERS, 8, SLOT), F32),
            vmem((NP, 8, SLOT), F32),
            vmem((REDUCERS, 8, SLOT), F32),
            sem((9,)),
            sem((NB, TILES)),
            sem((NB, TILES)),
            sem((TILES,)),
            sem((NB,)),
            sem((NB,)),
            sem,
            sem,
            sem,
            sem((GROUPS,)),
            sem,
            sem,
            sem((NB, TILES + 1)),
            sem((NB, TILES + 1)),
            sem((NB,)),
            sem((NB,)),
            sem((REDUCERS,)),
            sem,
            sem,
            sem((REDUCERS,)),
            sem,
        ],
        compiler_params=pltpu.CompilerParams(
            collective_id=0, has_side_effects=True, vmem_limit_bytes=62 * 1024 * 1024
        ),
    )(orbitals, trial_bands, potential, meta, *[jnp.asarray(held[name]) for name in TABLES])
    applied, intersection, projected = pl.pallas_call(
        finish,
        out_shape=(
            jax.ShapeDtypeStruct(trial_bands.shape, F32),
            jax.ShapeDtypeStruct((2, 32, SLOT), F32),
            jax.ShapeDtypeStruct((2, NB, 32), F32),
        ),
        in_specs=[vmem_spec, vmem_spec],
        out_specs=(vmem_spec, vmem_spec, vmem_spec),
    )(applied, final)
    return applied, intersection, jnp.swapaxes(projected, 1, 2)


def solution(mesh):
    return jax.shard_map(
        shards,
        mesh=mesh,
        in_specs=(
            P(None, "band", "plane", None),
            P(None, "band", "plane", None),
            P("plane", None, None),
            P("plane"),
            P("plane"),
        ),
        out_specs=(P(None, "band", "plane", None), P(None, "band", None), P(None, "band", None)),
        check_vma=False,
    )
```

```python
import functools
import math

import jax
import jax.numpy as jnp
import ml_dtypes
import numpy as np
from jax import lax
from jax.experimental import pallas as pl
from jax.experimental.pallas import tpu as pltpu
from jax.sharding import PartitionSpec as P

MESH = pl.DeviceIdType.MESH
BF16 = jnp.bfloat16
F32 = jnp.float32

GRID = 320
SLOT = 128
RADIUS = 63
NB = 4
NP = 32
SD = 416
ZP = GRID // NP
KZ = 2 * ZP
ROWS = 80
STICKS = NP * SD
PAD = 384
TILES = 6
EXTRA = 8 * SLOT
GROUP = 4 * SD
GROUPS = NP // 4
REDUCERS = 10


def split(table):
    table = np.asarray(table, np.float32)
    high = table.astype(ml_dtypes.bfloat16)
    low = (table - high.astype(np.float32)).astype(ml_dtypes.bfloat16)
    return high, low


@functools.lru_cache
def tables():
    half = SLOT // 2
    phase = np.outer(np.arange(SLOT) - half, np.arange(GRID)) % GRID
    cos, sin = np.cos(2 * math.pi / GRID * phase), np.sin(2 * math.pi / GRID * phase)
    full = np.zeros((NP, KZ, 2, SLOT))
    for q in range(NP):
        c, s = cos[:, q * ZP : (q + 1) * ZP].T, sin[:, q * ZP : (q + 1) * ZP].T
        full[q, :ZP, 0], full[q, :ZP, 1] = c, -s
        full[q, ZP:, 0], full[q, ZP:, 1] = s, c
    main = full[:, :16].reshape(NP * 16, 2 * SLOT)
    rest = np.tile(full[:, 16:], (1, 4, 1, 1)).reshape(NP * 16, 2 * SLOT)
    z_out = np.stack([*split(main), *split(rest)])
    z_back = np.stack([*split(main.T / GRID), *split(rest.T / GRID)])
    x_out = np.zeros((2, SLOT, 2, PAD))
    x_out[0, :, 0, :GRID], x_out[0, :, 1, :GRID] = cos, sin
    x_out[1, :, 0, :GRID], x_out[1, :, 1, :GRID] = -sin, cos
    x_out = x_out.reshape(2 * SLOT, 2 * PAD)
    y_out = np.block([[cos.T, -sin.T], [sin.T, cos.T]])
    low = ml_dtypes.bfloat16
    return dict(
        z_out=z_out,
        z_back=z_back,
        x_out=x_out.astype(low),
        y_out=y_out.astype(low),
        y_back=(y_out.T / GRID).astype(low),
        x_back=(x_out.T / GRID).astype(low),
        swap=np.eye(256).reshape(16, 16, 256).transpose(1, 0, 2).reshape(256, 256).astype(low),
    )


TABLES = ("z_out", "z_back", "x_out", "y_out", "y_back", "x_back", "swap")


def dot(first, second):
    return jnp.dot(first, second, preferred_element_type=F32)


def dot_nt(first, second):
    return lax.dot_general(first, second, (((1,), (1,)), ((), ())), preferred_element_type=F32)


def kernel(
    orbitals, trial_h, potential, columns_h, lengths_h, z_out_h, z_back_h, x_out_h, y_out_h, y_back_h, x_back_h, swap_h,
    applied_out, final_out,
    z_out, z_back, x_out, y_out, y_back, x_back, swap, pot, trial, columns, lengths,
    shares, masked, cols_out, cols_in, tx, rx, tx2, rx2,
    spots, values, onehot, spread, window, back,
    xin, yin, prod, xback, inside_s, inside_low, kinetic_s, local_s, applied, applied_low, applied_in,
    turned, turned_applied, extra_raw, extra_out, extra_in, gram, proj,
    part_out, part_in, part_sum, red_in, fin,
    load_sem, share_send, share_recv, own_sem, extra_send, extra_recv, cols_send, cols_recv, tx_send, tx_recv, tx2_send, tx2_recv,
    app_send, app_recv, part_send, part_recv, red_send, red_recv, fin_send, fin_recv, out_sem, joined,
):
    b = lax.axis_index("band")
    p = lax.axis_index("plane")

    barrier = pltpu.get_barrier_semaphore()

    def plane_peer(i):
        return 4 * lax.rem(p // 4 + i // 4, GROUPS) + lax.rem(p + i, 4)

    row, seat = p // 8, lax.rem(p, 8)

    def row_peer(i):
        return 8 * row + lax.rem(seat + i, 8)

    for d in range(1, NB):
        pl.semaphore_signal(barrier, inc=1, device_id=(lax.rem(b + d, NB), p), device_id_type=MESH)
        pl.semaphore_signal(barrier, inc=1, device_id=(b, 8 * lax.rem(row + d, 4) + seat), device_id_type=MESH)

    def greet(i, carry):
        pl.semaphore_signal(barrier, inc=1, device_id=(b, row_peer(i)), device_id_type=MESH)
        return carry

    lax.fori_loop(1, 8, greet, 0)
    loads = [
        pltpu.make_async_copy(source, target, load_sem.at[i])
        for i, (source, target) in enumerate([(columns_h, columns), (lengths_h, lengths), (trial_h, trial)])
    ]
    for load in loads:
        load.start()
    pl.semaphore_wait(barrier, 3 + 3 + 7)

    def tell(i, carry):
        pl.semaphore_signal(joined, inc=1, device_id=(b, row_peer(i)), device_id_type=MESH)
        return carry

    lax.fori_loop(1, 8, tell, 0)

    def share_rows(c, j):
        return pl.ds(pl.multiple_of((TILES * c + j) * 16, 16), 16)

    def share_copy(c, j, source):
        return pltpu.make_async_remote_copy(
            src_ref=orbitals.at[:, :, share_rows(c, j), :], dst_ref=shares.at[source, j],
            send_sem=share_send.at[c, j], recv_sem=share_recv.at[source, j],
            device_id=(c, p), device_id_type=MESH,
        )

    def own_copy(j):
        return pltpu.make_async_copy(orbitals.at[:, :, share_rows(b, j), :], shares.at[b, j], own_sem.at[j])

    def send_shares(j, carry):
        for d in range(1, NB):
            share_copy(lax.rem(b + d, NB), j, b).start()
        own_copy(j).start()
        return carry

    lax.fori_loop(0, TILES, send_shares, 0)

    loads += [
        pltpu.make_async_copy(source, target, load_sem.at[3 + i])
        for i, (source, target) in enumerate(
            [
                (z_out_h, z_out), (z_back_h, z_back), (x_out_h, x_out), (y_out_h, y_out), (y_back_h, y_back),
                (x_back_h, x_back), (swap_h, swap), (potential, pot),
                (orbitals.at[:, :, pl.ds(16 * 4 * TILES, 32), :], extra_raw),
            ]
        )
    ]
    for load in loads[3:]:
        load.start()
    for load in loads[:3]:
        load.wait()

    shift = 32 * lax.rem(p, 4)
    rest = 384 + pl.multiple_of(shift, 32)
    cols_out[0:4, :] = columns[...]
    cols_out[4:8, :] = jnp.zeros((4, SLOT), jnp.int32)
    cols_out[3:4, :] = pltpu.roll(cols_out[...], shift, 1)[3:4, :]
    slots = lax.broadcasted_iota(jnp.int32, (SLOT, SLOT), 1) - SLOT // 2
    for t in range(4):
        rows = SLOT if t < 3 else SD - 3 * SLOT
        as_column = jnp.broadcast_to(columns[t : t + 1, :].astype(F32), (SLOT, SLOT)).T.astype(jnp.int32)
        length = jnp.broadcast_to(lengths[t : t + 1, :].astype(F32), (SLOT, SLOT)).T.astype(jnp.int32)
        inside = (2 * jnp.abs(slots) < length).astype(F32)
        off_x, off_y = (as_column >> 7) - SLOT // 2, (as_column & 127) - SLOT // 2
        squared = off_x * off_x + off_y * off_y + slots * slots
        kinetic = squared.astype(F32) / F32(RADIUS * RADIUS)
        where = pl.ds(t * SLOT, rows)
        inside_s[where, :] = inside[:rows]
        kinetic_s[where, :] = kinetic[:rows]
    inside_low[...] = inside_s[...].astype(BF16)

    for k in range(2):
        masked[k, 384:512, :] = jnp.zeros((SLOT, SLOT), F32)
        masked[k, 0:384, :] = trial[k, 0, 0:384, :] * inside_s[0:384, :]
        masked[k, pl.ds(rest, 32), :] = trial[k, 0, 384:SD, :] * inside_s[384:SD, :]
    turned_trial = jnp.concatenate([masked[0].T, masked[1].T], axis=0)
    high = turned_trial.astype(BF16)
    low = (turned_trial - high.astype(F32)).astype(BF16)
    loads[3].wait()

    def z_dot(i):
        return dot(z_out[i], high) + (dot(z_out[i + 1], high) + dot(z_out[i], low))

    main = z_dot(0)
    for t in range(4):
        tx[:, 16 * t : 16 * t + 16, :] = main[:, t * SLOT : (t + 1) * SLOT].reshape(NP, 16, SLOT).astype(BF16)
    every = z_dot(2)
    quarter = (lax.broadcasted_iota(jnp.int32, (NP * 16, SLOT), 0) >> 2) & 3
    tail = jnp.zeros((NP * 16, SLOT), F32)
    for t in range(4):
        tail = jnp.where(quarter == t, every[:, t * SLOT : (t + 1) * SLOT], tail)
    tx[:, 64:80, :] = tail.reshape(NP, 16, SLOT).astype(BF16)

    def block_copy(q, source, out_ref, in_ref, send, recv):
        return pltpu.make_async_remote_copy(
            src_ref=out_ref.at[q], dst_ref=in_ref.at[source], send_sem=send, recv_sem=recv,
            device_id=(b, q), device_id_type=MESH,
        )

    def all_copies(out_ref, in_ref, send, recv, first=0, count=NP - 1):
        where = pl.ds(first, count)
        return pltpu.make_async_remote_copy(
            src_ref=out_ref.at[where], dst_ref=in_ref.at[where], send_sem=send, recv_sem=recv,
            device_id=(b, lax.rem(p + 1, NP)), device_id_type=MESH,
        )


    pl.semaphore_wait(joined, 7)

    def cols_copy(q, source):
        return pltpu.make_async_remote_copy(
            src_ref=cols_out, dst_ref=cols_in.at[source], send_sem=cols_send, recv_sem=cols_recv,
            device_id=(b, q), device_id_type=MESH,
        )

    def send_cols(i, carry):
        cols_copy(plane_peer(i), p).start()
        return carry

    lax.fori_loop(1, NP, send_cols, 0)

    def send_tx(i, carry):
        block_copy(plane_peer(i), p, tx, rx, tx_send, tx_recv.at[p // 4]).start()
        return carry

    lax.fori_loop(1, NP, send_tx, 0)
    cols_in[p] = cols_out[...]
    rx[p] = tx[p]

    gram[...] = jnp.zeros_like(gram)
    proj[...] = jnp.zeros_like(proj)

    def gram_step(j):
        own_copy(j).wait()
        for d in range(1, NB):
            c = lax.rem(b + d, NB)
            share_copy(c, j, c).wait_recv()
        mask = inside_low[share_rows(b, j), :]
        for k in range(2):
            for c in range(NB):
                halves = [
                    (shares[c, j, k, half * 16 : (half + 1) * 16] * mask[None]).reshape(256, SLOT) for half in range(2)
                ]
                flipped = dot(swap[...], jnp.concatenate(halves, axis=1)).astype(BF16)
                for half in range(2):
                    row = k * 128 + c * 32 + half * 16
                    for i in range(16):
                        lane = j * 2048 + i * SLOT
                        turned[row : row + 16, lane : lane + SLOT] = flipped[
                            i * 16 : i * 16 + 16, half * SLOT : (half + 1) * SLOT
                        ]
        block = turned[:, j * 2048 : (j + 1) * 2048]
        gram[...] += dot_nt(block, block)

    all_copies(cols_in, cols_in, cols_send, cols_recv).wait_recv()

    def group_lanes(g):
        return pl.ds(pl.multiple_of(g * GROUP, SLOT), GROUP)

    def fill_onehot(g, carry):
        where = group_lanes(g)
        pieces = [cols_in[4 * g + r, t : t + 1, :] for r in range(4) for t in range(3)]
        pieces.append(sum(cols_in[4 * g + r, 3:4, :] for r in range(1, 4)) + cols_in[4 * g, 3:4, :])
        group_cols = jnp.concatenate(pieces, axis=1)
        col_y = group_cols & 127
        spot = ((col_y >> 5) << 7) + (group_cols >> 7)
        spots[0:1, where] = col_y & 31
        for r in range(4):
            ids = lax.broadcasted_iota(jnp.int32, (SLOT, GROUP), 0) + r * SLOT
            onehot[r * SLOT : (r + 1) * SLOT, where] = (ids == spot).astype(F32).astype(BF16)
        return carry

    lax.fori_loop(0, GROUPS, fill_onehot, 0)

    window[...] = jnp.zeros_like(window)

    def to_window(i, carry):
        g = lax.rem(p // 4 + GROUPS - i, GROUPS)
        where = group_lanes(g)

        @pl.when(i == 0)
        def _():
            all_copies(tx, rx, tx_send, tx_recv.at[g], 0, 3).wait_recv()

        @pl.when(i > 0)
        def _():
            all_copies(tx, rx, tx_send, tx_recv.at[g], 0, 4).wait_recv()

        rest_block = jnp.zeros((32, SLOT), F32)
        for r in range(4):
            block = rx[4 * g + r].astype(F32)
            for t in range(3):
                lane = (3 * r + t) * SLOT
                values[0:16, lane : lane + SLOT] = block[16 * t : 16 * t + 16]
                values[16:20, lane : lane + SLOT] = block[64 + 4 * t : 68 + 4 * t]
            rest_block = rest_block + block[48:80]
        values[0:16, 12 * SLOT : GROUP] = rest_block[0:16]
        values[16:20, 12 * SLOT : GROUP] = rest_block[28:32]
        here = lax.broadcasted_iota(jnp.int32, (32, GROUP), 0) == spots[0:1, where]
        for r in range(KZ):
            spread[r * 32 : (r + 1) * 32, :] = jnp.where(here, values[r : r + 1, :], 0.0).astype(BF16)
        window[...] += dot_nt(spread[...], onehot[:, where])
        return carry

    lax.fori_loop(0, GROUPS, to_window, 0)

    loads[9].wait()
    loads[11].wait()
    for t in range(2):
        mask = inside_low[384 + 16 * t : 400 + 16 * t, :]
        for k in range(2):
            halves = [
                (extra_raw[k, half * 16 : (half + 1) * 16, 16 * t : 16 * t + 16] * mask[None]).reshape(256, SLOT)
                for half in range(2)
            ]
            flipped = dot(swap[...], jnp.concatenate(halves, axis=1)).astype(BF16)
            for half in range(2):
                for i in range(16):
                    lane = (16 * t + i) * SLOT
                    extra_out[k, half * 16 : half * 16 + 16, lane : lane + SLOT] = flipped[
                        i * 16 : i * 16 + 16, half * SLOT : (half + 1) * SLOT
                    ]

    def extra_copy(c, source):
        return pltpu.make_async_remote_copy(
            src_ref=extra_out.at[:, :, pl.ds(pl.multiple_of(c * EXTRA, EXTRA), EXTRA)], dst_ref=extra_in.at[source],
            send_sem=extra_send.at[c], recv_sem=extra_recv.at[source], device_id=(c, p), device_id_type=MESH,
        )

    gram_step(0)

    for load in loads[5:9]:
        load.wait()
    loads[10].wait()
    prod[...] = jnp.zeros_like(prod)

    def planes(i, carry):
        for h in range(2):
            z = 2 * i + h
            for k in range(2):
                for v in range(4):
                    piece = window[pl.ds(pl.multiple_of((k * ZP + z) * 32, 32), 32), v * SLOT : (v + 1) * SLOT]
                    rows = h * SLOT + v * 32
                    xin[rows : rows + 32, k * SLOT : (k + 1) * SLOT] = piece.astype(BF16)
        along_x = dot(xin[...], x_out[...])
        for h in range(2):
            for k in range(2):
                piece = along_x[h * SLOT : (h + 1) * SLOT, k * PAD : (k + 1) * PAD]
                yin[k * SLOT : (k + 1) * SLOT, h * PAD : (h + 1) * PAD] = piece.astype(BF16)
        spatial = dot(y_out[...], yin[...])
        for h in range(2):
            field = pot[2 * i + h]
            for k in range(2):
                piece = spatial[k * GRID : (k + 1) * GRID, h * PAD : h * PAD + GRID]
                prod[k * GRID : (k + 1) * GRID, h * PAD : h * PAD + GRID] = (piece * field).astype(BF16)
        back_y = dot(y_back[...], prod[...])
        for h in range(2):
            for k in range(2):
                piece = back_y[k * SLOT : (k + 1) * SLOT, h * PAD : (h + 1) * PAD]
                xback[h * SLOT : (h + 1) * SLOT, k * PAD : (k + 1) * PAD] = piece.astype(BF16)
        back_x = dot(xback[...], x_back[...])
        for h in range(2):
            z = 2 * i + h
            for k in range(2):
                for v in range(4):
                    rows = h * SLOT + v * 32
                    piece = back_x[rows : rows + 32, k * SLOT : (k + 1) * SLOT]
                    where = pl.ds(pl.multiple_of((k * ZP + z) * 32, 32), 32)
                    back[where, v * SLOT : (v + 1) * SLOT] = piece.astype(BF16)
        return carry

    lax.fori_loop(0, ZP // 2, planes, 0)

    gram_step(1)

    def from_window(i, carry):
        g = lax.rem(p // 4 + 1 + i, GROUPS)
        where = group_lanes(g)
        here = lax.broadcasted_iota(jnp.int32, (32, GROUP), 0) == spots[0:1, where]
        found = dot(back[...], onehot[:, where])
        for r in range(KZ):
            picked = jnp.where(here, found[r * 32 : (r + 1) * 32], 0.0)
            values[r : r + 1, :] = jnp.sum(picked, axis=0, keepdims=True)
        for r in range(4):
            q = 4 * g + r
            lanes = [slice((3 * r + t) * SLOT, (3 * r + t + 1) * SLOT) for t in range(3)] + [slice(12 * SLOT, GROUP)]
            for t in range(4):
                tx2[q, 16 * t : 16 * t + 16, :] = values[0:16, lanes[t]].astype(BF16)
            tx2[q, 64:80, :] = jnp.concatenate([values[16:20, lane] for lane in lanes], axis=0).astype(BF16)

        def send_back(r, carry):
            q = 4 * g + r

            @pl.when(q != p)
            def _():
                block_copy(q, p, tx2, rx2, tx2_send, tx2_recv).start()

            return carry

        lax.fori_loop(0, 4, send_back, 0)
        return carry

    lax.fori_loop(0, GROUPS, from_window, 0)
    rx2[p] = tx2[p]
    gram_step(2)

    all_copies(tx2, rx2, tx2_send, tx2_recv).wait_recv()

    loads[4].wait()
    rest_low = rx2[:, 64:80, :].reshape(NP * 16, SLOT).astype(F32)
    for t in range(4):
        first = rx2[:, 16 * t : 16 * t + 16, :].reshape(NP * 16, SLOT)
        second = jnp.where(quarter == t, rest_low, 0.0).astype(BF16)
        turned_local = (dot(z_back[0], first) + dot(z_back[2], second)) + (
            dot(z_back[1], first) + dot(z_back[3], second)
        )
        for k in range(2):
            local_s[k, t * SLOT : (t + 1) * SLOT, :] = turned_local[k * SLOT : (k + 1) * SLOT].T
    for k in range(2):
        for where, source in ((slice(0, 384), slice(0, 384)), (slice(384, SD), pl.ds(rest, 32))):
            kept = inside_s[where, :] * (kinetic_s[where, :] * trial[k, 0, where, :] + local_s[k, source, :])
            applied[k, 0, where, :] = kept
            applied_low[k, where, :] = kept.astype(BF16)
    applied_write = pltpu.make_async_copy(applied, applied_out, out_sem)
    applied_write.start()

    def app_rows(c, j):
        if j < TILES:
            return share_rows(c, j)
        return pl.ds(pl.multiple_of((4 * TILES + c // 2) * 16, 16), 16)

    def app_copy(c, j, source):
        return pltpu.make_async_remote_copy(
            src_ref=applied_low.at[:, app_rows(c, j), :], dst_ref=applied_in.at[j, source],
            send_sem=app_send.at[c, j], recv_sem=app_recv.at[source, j],
            device_id=(c, p), device_id_type=MESH,
        )

    for j in range(TILES + 1):
        for d in range(1, NB):
            app_copy(lax.rem(b + d, NB), j, b).start()
        applied_in[j, b] = applied_low[:, app_rows(b, j), :]
    for d in range(1, NB):
        extra_copy(lax.rem(b + d, NB), b).start()
    extra_in[b] = extra_out[:, :, pl.ds(pl.multiple_of(b * EXTRA, EXTRA), EXTRA)]
    gram_step(3)
    gram_step(4)

    def applied_rows(j):
        for d in range(1, NB):
            c = lax.rem(b + d, NB)
            app_copy(c, j, c).wait_recv()
        empty = jnp.zeros((4, 16, SLOT), BF16)
        pieces = [applied_in[j, c, k][None] for k in range(2) for c in range(NB)]
        gathered = jnp.concatenate(pieces[:4] + [empty] + pieces[4:] + [empty], axis=0).reshape(256, SLOT)
        flipped = dot(swap[...], gathered).astype(BF16)
        for i in range(16):
            turned_applied[:, i * SLOT : (i + 1) * SLOT] = flipped[i * 16 : i * 16 + 16]

    def applied_step(j):
        applied_rows(j)
        proj[...] += dot_nt(turned_applied[...], turned[:, j * 2048 : (j + 1) * 2048])

    for j in range(5):
        applied_step(j)
    gram_step(5)
    applied_step(5)
    for d in range(1, NB):
        c = lax.rem(b + d, NB)
        extra_copy(c, c).wait_recv()
    extra = jnp.concatenate([extra_in[c, k] for k in range(2) for c in range(NB)], axis=0)
    gram[...] += dot_nt(extra, extra)
    applied_rows(TILES)
    half = pl.ds(pl.multiple_of(lax.rem(b, 2) * EXTRA, EXTRA), EXTRA)
    proj[...] += dot_nt(turned_applied[:, half], extra)

    real = gram[0:128, 0:128] + gram[128:256, 128:256]
    imag = gram[0:128, 128:256] - gram[128:256, 0:128]
    proj_real = proj[0:8, 0:128] + proj[8:16, 128:256]
    proj_imag = proj[8:16, 0:128] - proj[0:8, 128:256]
    for c in range(NB):
        part_out[c, 0:32, :] = real[c * 32 : (c + 1) * 32]
        part_out[c, 32:64, :] = imag[c * 32 : (c + 1) * 32]
        part_out[c, 64:72, :] = proj_real
        part_out[c, 72:80, :] = proj_imag

    def part_copy(c, source):
        return pltpu.make_async_remote_copy(
            src_ref=part_out.at[c], dst_ref=part_in.at[source], send_sem=part_send.at[c], recv_sem=part_recv.at[source],
            device_id=(c, p), device_id_type=MESH,
        )

    for d in range(1, NB):
        part_copy(lax.rem(b + d, NB), b).start()
    part_in[b] = part_out[b]
    for d in range(1, NB):
        c = lax.rem(b + d, NB)
        part_copy(c, c).wait_recv()
    part_sum[...] = ((part_in[0] + part_in[1]) + (part_in[2] + part_in[3])).reshape(REDUCERS, 8, SLOT)

    def red_copy(t):
        return pltpu.make_async_remote_copy(
            src_ref=part_sum.at[t], dst_ref=red_in.at[p], send_sem=red_send.at[t], recv_sem=red_recv,
            device_id=(b, 3 * t), device_id_type=MESH,
        )

    def fin_copy(t, q):
        return pltpu.make_async_remote_copy(
            src_ref=fin.at[t], dst_ref=fin.at[t], send_sem=fin_send, recv_sem=fin_recv.at[t],
            device_id=(b, q), device_id_type=MESH,
        )

    mine = p // 3
    reducer = jnp.logical_and(lax.rem(p, 3) == 0, mine < REDUCERS)

    def send_red(t, carry):
        @pl.when(3 * t != p)
        def _():
            red_copy(t).start()

        return carry

    lax.fori_loop(0, REDUCERS, send_red, 0)

    @pl.when(reducer)
    def _():
        red_in[p] = part_sum[mine]
        all_copies(red_in, red_in, fin_send, red_recv).wait_recv()
        fin[mine] = jnp.sum(red_in[...], axis=0)

        def send_fin(i, carry):
            fin_copy(mine, plane_peer(i)).start()
            return carry

        lax.fori_loop(1, NP, send_fin, 0)

    def wait_fin(t, carry):
        @pl.when(3 * t != p)
        def _():
            fin_copy(t, 3 * t).wait_recv()

        return carry

    lax.fori_loop(0, REDUCERS, wait_fin, 0)
    final_out[...] = fin[...]

    all_copies(cols_in, cols_in, cols_send, cols_recv).wait_send()
    all_copies(tx, rx, tx_send, tx_recv.at[0]).wait_send()
    all_copies(tx2, rx2, tx2_send, tx2_recv).wait_send()

    @pl.when(reducer)
    def _():
        all_copies(red_in, red_in, fin_send, red_recv).wait_send()

    def red_sent(t, carry):
        @pl.when(3 * t != p)
        def _():
            red_copy(t).wait_send()

        return carry

    lax.fori_loop(0, REDUCERS, red_sent, 0)
    for d in range(1, NB):
        c = lax.rem(b + d, NB)
        extra_copy(c, b).wait_send()
        part_copy(c, b).wait_send()
        for j in range(TILES):
            share_copy(c, j, b).wait_send()
        for j in range(TILES + 1):
            app_copy(c, j, b).wait_send()
    applied_write.wait()


def finish(applied, final, applied_out, intersection, projected):
    applied_out[...] = applied[...]
    shift = lax.rem(SLOT - lax.axis_index("band") * 32, SLOT)
    for k in range(2):
        for r in range(4):
            intersection[k, 8 * r : 8 * r + 8, :] = final[4 * k + r]
        projected[k] = pltpu.roll(final[8 + k], shift, 1)[0:NB, 0:32]


def shards(orbitals, trial_bands, potential, stick_column, stick_length):
    pad = (0, 4 * SLOT - SD)
    columns = jnp.pad(stick_column, pad).reshape(4, SLOT)
    lengths = jnp.pad(stick_length, pad).reshape(4, SLOT)
    held = tables()
    any_spec = pl.BlockSpec(memory_space=pl.ANY)
    vmem_spec = pl.BlockSpec(memory_space=pltpu.VMEM)
    vmem = pltpu.VMEM
    sem = pltpu.SemaphoreType.DMA
    applied, final = pl.pallas_call(
        kernel,
        out_shape=(
            jax.ShapeDtypeStruct(trial_bands.shape, F32),
            jax.ShapeDtypeStruct((REDUCERS, 8, SLOT), F32),
        ),
        in_specs=[any_spec] * (5 + len(TABLES)),
        out_specs=(any_spec, vmem_spec),
        scratch_shapes=[vmem(held[name].shape, BF16) for name in TABLES]
        + [
            vmem((ZP, GRID, GRID), F32),
            vmem((2, 1, SD, SLOT), F32),
            vmem((4, SLOT), jnp.int32),
            vmem((4, SLOT), jnp.int32),
            vmem((NB, TILES, 2, 32, 16, SLOT), BF16),
            vmem((2, 512, SLOT), F32),
            vmem((8, SLOT), jnp.int32),
            vmem((NP, 8, SLOT), jnp.int32),
            vmem((NP, ROWS, SLOT), BF16),
            vmem((NP, ROWS, SLOT), BF16),
            vmem((NP, ROWS, SLOT), BF16),
            vmem((NP, ROWS, SLOT), BF16),
            vmem((8, STICKS), jnp.int32),
            vmem((24, GROUP), F32),
            vmem((4 * SLOT, STICKS), BF16),
            vmem((KZ * 32, GROUP), BF16),
            vmem((KZ * 32, 4 * SLOT), F32),
            vmem((KZ * 32, 4 * SLOT), BF16),
            vmem((2 * SLOT, 2 * SLOT), BF16),
            vmem((2 * SLOT, 2 * PAD), BF16),
            vmem((2 * GRID, 2 * PAD), BF16),
            vmem((2 * SLOT, 2 * PAD), BF16),
            vmem((SD, SLOT), F32),
            vmem((SD, SLOT), BF16),
            vmem((SD, SLOT), F32),
            vmem((2, 512, SLOT), F32),
            vmem((2, 1, SD, SLOT), F32),
            vmem((2, SD, SLOT), BF16),
            vmem((TILES + 1, NB, 2, 16, SLOT), BF16),
            vmem((256, TILES * 2048), BF16),
            vmem((16, 2048), BF16),
            vmem((2, 32, 32, SLOT), BF16),
            vmem((2, 32, 32 * SLOT), BF16),
            vmem((NB, 2, 32, EXTRA), BF16),
            vmem((256, 256), F32),
            vmem((16, 256), F32),
            vmem((NB, 80, SLOT), F32),
            vmem((NB, 80, SLOT), F32),
            vmem((REDUCERS, 8, SLOT), F32),
            vmem((NP, 8, SLOT), F32),
            vmem((REDUCERS, 8, SLOT), F32),
            sem((12,)),
            sem((NB, TILES)),
            sem((NB, TILES)),
            sem((TILES,)),
            sem((NB,)),
            sem((NB,)),
            sem,
            sem,
            sem,
            sem((GROUPS,)),
            sem,
            sem,
            sem((NB, TILES + 1)),
            sem((NB, TILES + 1)),
            sem((NB,)),
            sem((NB,)),
            sem((REDUCERS,)),
            sem,
            sem,
            sem((REDUCERS,)),
            sem,
            pltpu.SemaphoreType.REGULAR,
        ],
        compiler_params=pltpu.CompilerParams(
            collective_id=0, has_side_effects=True, vmem_limit_bytes=62 * 1024 * 1024
        ),
    )(orbitals, trial_bands, potential, columns, lengths, *[jnp.asarray(held[name]) for name in TABLES])
    applied, intersection, projected = pl.pallas_call(
        finish,
        out_shape=(
            jax.ShapeDtypeStruct(trial_bands.shape, F32),
            jax.ShapeDtypeStruct((2, 32, SLOT), F32),
            jax.ShapeDtypeStruct((2, NB, 32), F32),
        ),
        in_specs=[vmem_spec, vmem_spec],
        out_specs=(vmem_spec, vmem_spec, vmem_spec),
    )(applied, final)
    return applied, intersection, jnp.swapaxes(projected, 1, 2)


def solution(mesh):
    return jax.shard_map(
        shards,
        mesh=mesh,
        in_specs=(
            P(None, "band", "plane", None),
            P(None, "band", "plane", None),
            P("plane", None, None),
            P("plane"),
            P("plane"),
        ),
        out_specs=(P(None, "band", "plane", None), P(None, "band", None), P(None, "band", None)),
        check_vma=False,
    )
```

```python
import functools
import math

import jax
import jax.numpy as jnp
import ml_dtypes
import numpy as np
from jax import lax
from jax.experimental import pallas as pl
from jax.experimental.pallas import tpu as pltpu
from jax.sharding import PartitionSpec as P

MESH = pl.DeviceIdType.MESH
BF16 = jnp.bfloat16
F32 = jnp.float32

GRID = 320
SLOT = 128
RADIUS = 63
NB = 4
NP = 32
SD = 416
ZP = GRID // NP
KZ = 2 * ZP
ROWS = 80
STICKS = NP * SD
PAD = 384
TILES = 6
EXTRA = 8 * SLOT
GROUP = 4 * SD
GROUPS = NP // 4
SUMS = 24


def split(table):
    table = np.asarray(table, np.float32)
    high = table.astype(ml_dtypes.bfloat16)
    low = (table - high.astype(np.float32)).astype(ml_dtypes.bfloat16)
    return high, low


@functools.lru_cache
def tables():
    half = SLOT // 2
    phase = np.outer(np.arange(SLOT) - half, np.arange(GRID)) % GRID
    cos, sin = np.cos(2 * math.pi / GRID * phase), np.sin(2 * math.pi / GRID * phase)
    full = np.zeros((NP, KZ, 2, SLOT))
    for q in range(NP):
        c, s = cos[:, q * ZP : (q + 1) * ZP].T, sin[:, q * ZP : (q + 1) * ZP].T
        full[q, :ZP, 0], full[q, :ZP, 1] = c, -s
        full[q, ZP:, 0], full[q, ZP:, 1] = s, c
    main = full[:, :16].reshape(NP * 16, 2 * SLOT)
    rest = np.tile(full[:, 16:], (1, 4, 1, 1)).reshape(NP * 16, 2 * SLOT)
    z_out = np.stack([*split(main), *split(rest)])
    z_back = np.stack([*split(main.T / GRID), *split(rest.T / GRID)])
    x_out = np.zeros((2, SLOT, 2, PAD))
    x_out[0, :, 0, :GRID], x_out[0, :, 1, :GRID] = cos, sin
    x_out[1, :, 0, :GRID], x_out[1, :, 1, :GRID] = -sin, cos
    x_out = x_out.reshape(2 * SLOT, 2 * PAD)
    y_out = np.block([[cos.T, -sin.T], [sin.T, cos.T]])
    low = ml_dtypes.bfloat16
    return dict(
        z_out=z_out,
        z_back=z_back,
        x_out=x_out.astype(low),
        y_out=y_out.astype(low),
        y_back=(y_out.T / GRID).astype(low),
        x_back=(x_out.T / GRID).astype(low),
        swap=np.eye(256).reshape(16, 16, 256).transpose(1, 0, 2).reshape(256, 256).astype(low),
    )


TABLES = ("z_out", "z_back", "x_out", "y_out", "y_back", "x_back", "swap")


def dot(first, second):
    return jnp.dot(first, second, preferred_element_type=F32)


def dot_nt(first, second):
    return lax.dot_general(first, second, (((1,), (1,)), ((), ())), preferred_element_type=F32)


def kernel(
    orbitals, trial_h, potential, columns, lengths, z_out_h, z_back_h, x_out_h, y_out_h, y_back_h, x_back_h, swap_h,
    applied_out, final_out,
    z_out, z_back, x_out, y_out, y_back, x_back, swap, pot, trial,
    shares, masked, cols_out, cols_in, tx, rx, tx2, rx2,
    spots, values, onehot, spread, window, back,
    xin, yin, prod, xback, inside_s, inside_low, kinetic_s, local_s, applied, applied_low, applied_in,
    turned, turned_applied, extra_raw, extra_out, extra_in, gram, proj,
    sum_out, sum_in, row_out, row_in, fin,
    load_sem, share_send, share_recv, own_sem, extra_send, extra_recv, cols_send, cols_recv, tx_send, tx_recv, tx2_send, tx2_recv,
    app_send, app_recv, sum_send, sum_recv, row_send, row_recv, fin_send, fin_recv, out_sem, joined,
):
    b = lax.axis_index("band")
    p = lax.axis_index("plane")

    barrier = pltpu.get_barrier_semaphore()

    def plane_peer(i):
        return 4 * lax.rem(p // 4 + i // 4, GROUPS) + lax.rem(p + i, 4)

    row, seat = p // 8, lax.rem(p, 8)

    def row_peer(i):
        return 8 * row + lax.rem(seat + i, 8)

    for d in range(1, NB):
        pl.semaphore_signal(barrier, inc=1, device_id=(lax.rem(b + d, NB), p), device_id_type=MESH)
        pl.semaphore_signal(barrier, inc=1, device_id=(b, 8 * lax.rem(row + d, 4) + seat), device_id_type=MESH)

    def greet(i, carry):
        pl.semaphore_signal(barrier, inc=1, device_id=(b, row_peer(i)), device_id_type=MESH)
        return carry

    lax.fori_loop(1, 8, greet, 0)
    loads = [pltpu.make_async_copy(trial_h, trial, load_sem.at[0])]
    for load in loads:
        load.start()
    pl.semaphore_wait(barrier, 3 + 3 + 7)

    def tell(i, carry):
        pl.semaphore_signal(joined, inc=1, device_id=(b, row_peer(i)), device_id_type=MESH)
        return carry

    lax.fori_loop(1, 8, tell, 0)

    def share_rows(c, j):
        return pl.ds(pl.multiple_of((TILES * c + j) * 16, 16), 16)

    def share_copy(c, j, source):
        return pltpu.make_async_remote_copy(
            src_ref=orbitals.at[:, :, share_rows(c, j), :], dst_ref=shares.at[source, j],
            send_sem=share_send.at[c, j], recv_sem=share_recv.at[source, j],
            device_id=(c, p), device_id_type=MESH,
        )

    def own_copy(j):
        return pltpu.make_async_copy(orbitals.at[:, :, share_rows(b, j), :], shares.at[b, j], own_sem.at[j])

    def send_shares(j, carry):
        for d in range(1, NB):
            share_copy(lax.rem(b + d, NB), j, b).start()
        own_copy(j).start()
        return carry

    lax.fori_loop(0, TILES, send_shares, 0)

    loads += [
        pltpu.make_async_copy(source, target, load_sem.at[1 + i])
        for i, (source, target) in enumerate(
            [
                (z_out_h, z_out), (z_back_h, z_back), (x_out_h, x_out), (y_out_h, y_out), (y_back_h, y_back),
                (x_back_h, x_back), (swap_h, swap), (potential, pot),
                (orbitals.at[:, :, pl.ds(16 * 4 * TILES, 32), :], extra_raw),
            ]
        )
    ]
    for load in loads[1:]:
        load.start()
    loads[0].wait()

    shift = 32 * lax.rem(p, 4)
    rest = 384 + pl.multiple_of(shift, 32)
    short = jnp.zeros((1, 4 * SLOT - SD), jnp.int32)
    column_rows, length_rows = (
        [held[t * SLOT : (t + 1) * SLOT].reshape(1, SLOT) for t in range(3)]
        + [jnp.concatenate([held[3 * SLOT : SD].reshape(1, SD - 3 * SLOT), short], axis=1)]
        for held in (columns, lengths)
    )
    for t in range(4):
        cols_out[t : t + 1, :] = column_rows[t]
    cols_out[4:8, :] = jnp.zeros((4, SLOT), jnp.int32)
    cols_out[3:4, :] = pltpu.roll(cols_out[...], shift, 1)[3:4, :]
    slots = lax.broadcasted_iota(jnp.int32, (SLOT, SLOT), 1) - SLOT // 2
    for t in range(4):
        rows = SLOT if t < 3 else SD - 3 * SLOT
        as_column = jnp.broadcast_to(column_rows[t].astype(F32), (SLOT, SLOT)).T.astype(jnp.int32)
        length = jnp.broadcast_to(length_rows[t].astype(F32), (SLOT, SLOT)).T.astype(jnp.int32)
        inside = (2 * jnp.abs(slots) < length).astype(F32)
        off_x, off_y = (as_column >> 7) - SLOT // 2, (as_column & 127) - SLOT // 2
        squared = off_x * off_x + off_y * off_y + slots * slots
        kinetic = squared.astype(F32) / F32(RADIUS * RADIUS)
        where = pl.ds(t * SLOT, rows)
        inside_s[where, :] = inside[:rows]
        kinetic_s[where, :] = kinetic[:rows]
    inside_low[...] = inside_s[...].astype(BF16)

    for k in range(2):
        masked[k, 384:512, :] = jnp.zeros((SLOT, SLOT), F32)
        masked[k, 0:384, :] = trial[k, 0, 0:384, :] * inside_s[0:384, :]
        masked[k, pl.ds(rest, 32), :] = trial[k, 0, 384:SD, :] * inside_s[384:SD, :]
    turned_trial = jnp.concatenate([masked[0].T, masked[1].T], axis=0)
    high = turned_trial.astype(BF16)
    low = (turned_trial - high.astype(F32)).astype(BF16)
    loads[1].wait()

    def z_dot(i):
        return dot(z_out[i], high) + (dot(z_out[i + 1], high) + dot(z_out[i], low))

    main = z_dot(0)
    for t in range(4):
        tx[:, 16 * t : 16 * t + 16, :] = main[:, t * SLOT : (t + 1) * SLOT].reshape(NP, 16, SLOT).astype(BF16)
    every = z_dot(2)
    quarter = (lax.broadcasted_iota(jnp.int32, (NP * 16, SLOT), 0) >> 2) & 3
    tail = jnp.zeros((NP * 16, SLOT), F32)
    for t in range(4):
        tail = jnp.where(quarter == t, every[:, t * SLOT : (t + 1) * SLOT], tail)
    tx[:, 64:80, :] = tail.reshape(NP, 16, SLOT).astype(BF16)

    def block_copy(q, source, out_ref, in_ref, send, recv):
        return pltpu.make_async_remote_copy(
            src_ref=out_ref.at[q], dst_ref=in_ref.at[source], send_sem=send, recv_sem=recv,
            device_id=(b, q), device_id_type=MESH,
        )

    def all_copies(out_ref, in_ref, send, recv, first=0, count=NP - 1):
        where = pl.ds(first, count)
        return pltpu.make_async_remote_copy(
            src_ref=out_ref.at[where], dst_ref=in_ref.at[where], send_sem=send, recv_sem=recv,
            device_id=(b, lax.rem(p + 1, NP)), device_id_type=MESH,
        )


    pl.semaphore_wait(joined, 7)

    def cols_copy(q, source):
        return pltpu.make_async_remote_copy(
            src_ref=cols_out, dst_ref=cols_in.at[source], send_sem=cols_send, recv_sem=cols_recv,
            device_id=(b, q), device_id_type=MESH,
        )

    def send_cols(i, carry):
        cols_copy(plane_peer(i), p).start()
        return carry

    lax.fori_loop(1, NP, send_cols, 0)

    def send_tx(i, carry):
        block_copy(plane_peer(i), p, tx, rx, tx_send, tx_recv.at[p // 4]).start()
        return carry

    lax.fori_loop(1, NP, send_tx, 0)
    cols_in[p] = cols_out[...]
    rx[p] = tx[p]

    gram[...] = jnp.zeros_like(gram)
    proj[...] = jnp.zeros_like(proj)

    def gram_step(j):
        own_copy(j).wait()
        for d in range(1, NB):
            c = lax.rem(b + d, NB)
            share_copy(c, j, c).wait_recv()
        mask = inside_low[share_rows(b, j), :]
        for k in range(2):
            for c in range(NB):
                halves = [
                    (shares[c, j, k, half * 16 : (half + 1) * 16] * mask[None]).reshape(256, SLOT) for half in range(2)
                ]
                flipped = dot(swap[...], jnp.concatenate(halves, axis=1)).astype(BF16)
                for half in range(2):
                    row = k * 128 + c * 32 + half * 16
                    for i in range(16):
                        lane = j * 2048 + i * SLOT
                        turned[row : row + 16, lane : lane + SLOT] = flipped[
                            i * 16 : i * 16 + 16, half * SLOT : (half + 1) * SLOT
                        ]
        block = turned[:, j * 2048 : (j + 1) * 2048]
        gram[...] += dot_nt(block, block)

    all_copies(cols_in, cols_in, cols_send, cols_recv).wait_recv()

    def group_lanes(g):
        return pl.ds(pl.multiple_of(g * GROUP, SLOT), GROUP)

    def fill_onehot(g, carry):
        where = group_lanes(g)
        pieces = [cols_in[4 * g + r, t : t + 1, :] for r in range(4) for t in range(3)]
        pieces.append(sum(cols_in[4 * g + r, 3:4, :] for r in range(1, 4)) + cols_in[4 * g, 3:4, :])
        group_cols = jnp.concatenate(pieces, axis=1)
        col_y = group_cols & 127
        spot = ((col_y >> 5) << 7) + (group_cols >> 7)
        spots[0:1, where] = col_y & 31
        for r in range(4):
            ids = lax.broadcasted_iota(jnp.int32, (SLOT, GROUP), 0) + r * SLOT
            onehot[r * SLOT : (r + 1) * SLOT, where] = (ids == spot).astype(F32).astype(BF16)
        return carry

    lax.fori_loop(0, GROUPS, fill_onehot, 0)

    window[...] = jnp.zeros_like(window)

    def to_window(i, carry):
        g = lax.rem(p // 4 + GROUPS - i, GROUPS)
        where = group_lanes(g)

        @pl.when(i == 0)
        def _():
            all_copies(tx, rx, tx_send, tx_recv.at[g], 0, 3).wait_recv()

        @pl.when(i > 0)
        def _():
            all_copies(tx, rx, tx_send, tx_recv.at[g], 0, 4).wait_recv()

        rest_block = jnp.zeros((32, SLOT), F32)
        for r in range(4):
            block = rx[4 * g + r].astype(F32)
            for t in range(3):
                lane = (3 * r + t) * SLOT
                values[0:16, lane : lane + SLOT] = block[16 * t : 16 * t + 16]
                values[16:20, lane : lane + SLOT] = block[64 + 4 * t : 68 + 4 * t]
            rest_block = rest_block + block[48:80]
        values[0:16, 12 * SLOT : GROUP] = rest_block[0:16]
        values[16:20, 12 * SLOT : GROUP] = rest_block[28:32]
        here = lax.broadcasted_iota(jnp.int32, (32, GROUP), 0) == spots[0:1, where]
        for r in range(KZ):
            spread[r * 32 : (r + 1) * 32, :] = jnp.where(here, values[r : r + 1, :], 0.0).astype(BF16)
        window[...] += dot_nt(spread[...], onehot[:, where])
        return carry

    lax.fori_loop(0, GROUPS, to_window, 0)

    loads[7].wait()
    loads[9].wait()
    for t in range(2):
        mask = inside_low[384 + 16 * t : 400 + 16 * t, :]
        for k in range(2):
            halves = [
                (extra_raw[k, half * 16 : (half + 1) * 16, 16 * t : 16 * t + 16] * mask[None]).reshape(256, SLOT)
                for half in range(2)
            ]
            flipped = dot(swap[...], jnp.concatenate(halves, axis=1)).astype(BF16)
            for half in range(2):
                for i in range(16):
                    lane = (16 * t + i) * SLOT
                    extra_out[k, half * 16 : half * 16 + 16, lane : lane + SLOT] = flipped[
                        i * 16 : i * 16 + 16, half * SLOT : (half + 1) * SLOT
                    ]

    def extra_copy(c, source):
        return pltpu.make_async_remote_copy(
            src_ref=extra_out.at[:, :, pl.ds(pl.multiple_of(c * EXTRA, EXTRA), EXTRA)], dst_ref=extra_in.at[source],
            send_sem=extra_send.at[c], recv_sem=extra_recv.at[source], device_id=(c, p), device_id_type=MESH,
        )

    gram_step(0)

    for load in loads[3:7]:
        load.wait()
    loads[8].wait()
    prod[...] = jnp.zeros_like(prod)

    def planes(i, carry):
        for h in range(2):
            z = 2 * i + h
            for k in range(2):
                for v in range(4):
                    piece = window[pl.ds(pl.multiple_of((k * ZP + z) * 32, 32), 32), v * SLOT : (v + 1) * SLOT]
                    rows = h * SLOT + v * 32
                    xin[rows : rows + 32, k * SLOT : (k + 1) * SLOT] = piece.astype(BF16)
        along_x = dot(xin[...], x_out[...])
        for h in range(2):
            for k in range(2):
                piece = along_x[h * SLOT : (h + 1) * SLOT, k * PAD : (k + 1) * PAD]
                yin[k * SLOT : (k + 1) * SLOT, h * PAD : (h + 1) * PAD] = piece.astype(BF16)
        spatial = dot(y_out[...], yin[...])
        for h in range(2):
            field = pot[2 * i + h]
            for k in range(2):
                piece = spatial[k * GRID : (k + 1) * GRID, h * PAD : h * PAD + GRID]
                prod[k * GRID : (k + 1) * GRID, h * PAD : h * PAD + GRID] = (piece * field).astype(BF16)
        back_y = dot(y_back[...], prod[...])
        for h in range(2):
            for k in range(2):
                piece = back_y[k * SLOT : (k + 1) * SLOT, h * PAD : (h + 1) * PAD]
                xback[h * SLOT : (h + 1) * SLOT, k * PAD : (k + 1) * PAD] = piece.astype(BF16)
        back_x = dot(xback[...], x_back[...])
        for h in range(2):
            z = 2 * i + h
            for k in range(2):
                for v in range(4):
                    rows = h * SLOT + v * 32
                    piece = back_x[rows : rows + 32, k * SLOT : (k + 1) * SLOT]
                    where = pl.ds(pl.multiple_of((k * ZP + z) * 32, 32), 32)
                    back[where, v * SLOT : (v + 1) * SLOT] = piece.astype(BF16)
        return carry

    lax.fori_loop(0, ZP // 2, planes, 0)

    gram_step(1)

    def from_window(i, carry):
        g = lax.rem(p // 4 + 1 + i, GROUPS)
        where = group_lanes(g)
        here = lax.broadcasted_iota(jnp.int32, (32, GROUP), 0) == spots[0:1, where]
        found = dot(back[...], onehot[:, where])
        for r in range(KZ):
            picked = jnp.where(here, found[r * 32 : (r + 1) * 32], 0.0)
            values[r : r + 1, :] = jnp.sum(picked, axis=0, keepdims=True)
        for r in range(4):
            q = 4 * g + r
            lanes = [slice((3 * r + t) * SLOT, (3 * r + t + 1) * SLOT) for t in range(3)] + [slice(12 * SLOT, GROUP)]
            for t in range(4):
                tx2[q, 16 * t : 16 * t + 16, :] = values[0:16, lanes[t]].astype(BF16)
            tx2[q, 64:80, :] = jnp.concatenate([values[16:20, lane] for lane in lanes], axis=0).astype(BF16)

        def send_back(r, carry):
            q = 4 * g + r

            @pl.when(q != p)
            def _():
                block_copy(q, p, tx2, rx2, tx2_send, tx2_recv).start()

            return carry

        lax.fori_loop(0, 4, send_back, 0)
        return carry

    lax.fori_loop(0, GROUPS, from_window, 0)
    rx2[p] = tx2[p]
    gram_step(2)

    all_copies(tx2, rx2, tx2_send, tx2_recv).wait_recv()

    loads[2].wait()
    rest_low = rx2[:, 64:80, :].reshape(NP * 16, SLOT).astype(F32)
    for t in range(4):
        first = rx2[:, 16 * t : 16 * t + 16, :].reshape(NP * 16, SLOT)
        second = jnp.where(quarter == t, rest_low, 0.0).astype(BF16)
        turned_local = (dot(z_back[0], first) + dot(z_back[2], second)) + (
            dot(z_back[1], first) + dot(z_back[3], second)
        )
        for k in range(2):
            local_s[k, t * SLOT : (t + 1) * SLOT, :] = turned_local[k * SLOT : (k + 1) * SLOT].T
    for k in range(2):
        for where, source in ((slice(0, 384), slice(0, 384)), (slice(384, SD), pl.ds(rest, 32))):
            kept = inside_s[where, :] * (kinetic_s[where, :] * trial[k, 0, where, :] + local_s[k, source, :])
            applied[k, 0, where, :] = kept
            applied_low[k, where, :] = kept.astype(BF16)
    applied_write = pltpu.make_async_copy(applied, applied_out, out_sem)
    applied_write.start()

    def app_rows(c, j):
        if j < TILES:
            return share_rows(c, j)
        return pl.ds(pl.multiple_of((4 * TILES + c // 2) * 16, 16), 16)

    def app_copy(c, j, source):
        return pltpu.make_async_remote_copy(
            src_ref=applied_low.at[:, app_rows(c, j), :], dst_ref=applied_in.at[j, source],
            send_sem=app_send.at[c, j], recv_sem=app_recv.at[source, j],
            device_id=(c, p), device_id_type=MESH,
        )

    for j in range(TILES + 1):
        for d in range(1, NB):
            app_copy(lax.rem(b + d, NB), j, b).start()
        applied_in[j, b] = applied_low[:, app_rows(b, j), :]
    for d in range(1, NB):
        extra_copy(lax.rem(b + d, NB), b).start()
    extra_in[b] = extra_out[:, :, pl.ds(pl.multiple_of(b * EXTRA, EXTRA), EXTRA)]
    gram_step(3)
    gram_step(4)

    def applied_rows(j):
        for d in range(1, NB):
            c = lax.rem(b + d, NB)
            app_copy(c, j, c).wait_recv()
        empty = jnp.zeros((4, 16, SLOT), BF16)
        pieces = [applied_in[j, c, k][None] for k in range(2) for c in range(NB)]
        gathered = jnp.concatenate(pieces[:4] + [empty] + pieces[4:] + [empty], axis=0).reshape(256, SLOT)
        flipped = dot(swap[...], gathered).astype(BF16)
        for i in range(16):
            turned_applied[:, i * SLOT : (i + 1) * SLOT] = flipped[i * 16 : i * 16 + 16]

    def applied_step(j):
        applied_rows(j)
        proj[...] += dot_nt(turned_applied[...], turned[:, j * 2048 : (j + 1) * 2048])

    for j in range(5):
        applied_step(j)
    gram_step(5)
    applied_step(5)
    for d in range(1, NB):
        c = lax.rem(b + d, NB)
        extra_copy(c, c).wait_recv()
    extra = jnp.concatenate([extra_in[c, k] for k in range(2) for c in range(NB)], axis=0)
    gram[...] += dot_nt(extra, extra)
    applied_rows(TILES)
    half = pl.ds(pl.multiple_of(lax.rem(b, 2) * EXTRA, EXTRA), EXTRA)
    proj[...] += dot_nt(turned_applied[:, half], extra)

    real = gram[0:128, 0:128] + gram[128:256, 128:256]
    imag = gram[0:128, 128:256] - gram[128:256, 0:128]
    proj_real = proj[0:8, 0:128] + proj[8:16, 128:256]
    proj_imag = proj[8:16, 0:128] - proj[0:8, 128:256]
    both = jnp.concatenate([proj_real[0:NB], proj_imag[0:NB]], axis=0)
    for c in range(NB):
        for k, part in enumerate((real, imag)):
            for half in range(2):
                first = c * 32 + half * 16
                sum_out[4 * c + 2 * k + half, 0:16, :] = part[first : first + 16]
                sum_out[4 * c + 2 * k + half, 16:SUMS, :] = both
    own = 4 * b + row

    def sum_copy(i):
        to = lax.rem(own + i, 16)
        return pltpu.make_async_remote_copy(
            src_ref=sum_out.at[to], dst_ref=sum_in.at[own], send_sem=sum_send, recv_sem=sum_recv,
            device_id=(to // 4, 8 * lax.rem(to, 4) + seat), device_id_type=MESH,
        )

    def row_copy(i):
        return pltpu.make_async_remote_copy(
            src_ref=row_out, dst_ref=row_in.at[seat], send_sem=row_send, recv_sem=row_recv,
            device_id=(b, row_peer(i)), device_id_type=MESH,
        )

    def fin_copy(d):
        return pltpu.make_async_remote_copy(
            src_ref=fin.at[row], dst_ref=fin.at[row], send_sem=fin_send, recv_sem=fin_recv,
            device_id=(b, 8 * lax.rem(row + d, 4) + seat), device_id_type=MESH,
        )

    def send_sum(i, carry):
        sum_copy(i).start()
        return carry

    lax.fori_loop(1, 16, send_sum, 0)
    sum_in[own] = sum_out[own]
    sums_there = all_copies(sum_in, sum_in, sum_send, sum_recv, 0, 15)
    sums_there.wait_recv()
    row_out[...] = jnp.sum(sum_in[...], axis=0)

    def send_row(i, carry):
        row_copy(i).start()
        return carry

    lax.fori_loop(1, 8, send_row, 0)
    row_in[seat] = row_out[...]
    rows_there = all_copies(row_in, row_in, row_send, row_recv, 0, 7)
    rows_there.wait_recv()
    fin[row] = jnp.sum(row_in[...], axis=0)
    for d in range(1, 4):
        fin_copy(d).start()
    fin_there = all_copies(fin, fin, fin_send, fin_recv, 0, 3)
    fin_there.wait_recv()
    for r in range(4):
        final_out[2 * r] = fin[r, 0:8, :]
        final_out[2 * r + 1] = fin[r, 8:16, :]
    final_out[8] = fin[0, 16:SUMS, :]

    all_copies(cols_in, cols_in, cols_send, cols_recv).wait_send()
    all_copies(tx, rx, tx_send, tx_recv.at[0]).wait_send()
    all_copies(tx2, rx2, tx2_send, tx2_recv).wait_send()

    sums_there.wait_send()
    rows_there.wait_send()
    fin_there.wait_send()
    for d in range(1, NB):
        c = lax.rem(b + d, NB)
        extra_copy(c, b).wait_send()
        for j in range(TILES):
            share_copy(c, j, b).wait_send()
        for j in range(TILES + 1):
            app_copy(c, j, b).wait_send()
    applied_write.wait()


def finish(applied, final, applied_out, intersection, projected):
    applied_out[...] = applied[...]
    shift = lax.rem(SLOT - lax.axis_index("band") * 32, SLOT)
    for k in range(2):
        for r in range(4):
            intersection[k, 8 * r : 8 * r + 8, :] = final[4 * k + r]
        projected[k] = pltpu.roll(final[8], shift, 1)[NB * k : NB * k + NB, 0:32]


def shards(orbitals, trial_bands, potential, stick_column, stick_length):
    held = tables()
    any_spec = pl.BlockSpec(memory_space=pl.ANY)
    vmem_spec = pl.BlockSpec(memory_space=pltpu.VMEM)
    vmem = pltpu.VMEM
    sem = pltpu.SemaphoreType.DMA
    applied, final = pl.pallas_call(
        kernel,
        out_shape=(
            jax.ShapeDtypeStruct(trial_bands.shape, F32),
            jax.ShapeDtypeStruct((9, 8, SLOT), F32),
        ),
        in_specs=[any_spec] * 3 + [vmem_spec] * 2 + [any_spec] * len(TABLES),
        out_specs=(any_spec, vmem_spec),
        scratch_shapes=[vmem(held[name].shape, BF16) for name in TABLES]
        + [
            vmem((ZP, GRID, GRID), F32),
            vmem((2, 1, SD, SLOT), F32),
            vmem((NB, TILES, 2, 32, 16, SLOT), BF16),
            vmem((2, 512, SLOT), F32),
            vmem((8, SLOT), jnp.int32),
            vmem((NP, 8, SLOT), jnp.int32),
            vmem((NP, ROWS, SLOT), BF16),
            vmem((NP, ROWS, SLOT), BF16),
            vmem((NP, ROWS, SLOT), BF16),
            vmem((NP, ROWS, SLOT), BF16),
            vmem((8, STICKS), jnp.int32),
            vmem((24, GROUP), F32),
            vmem((4 * SLOT, STICKS), BF16),
            vmem((KZ * 32, GROUP), BF16),
            vmem((KZ * 32, 4 * SLOT), F32),
            vmem((KZ * 32, 4 * SLOT), BF16),
            vmem((2 * SLOT, 2 * SLOT), BF16),
            vmem((2 * SLOT, 2 * PAD), BF16),
            vmem((2 * GRID, 2 * PAD), BF16),
            vmem((2 * SLOT, 2 * PAD), BF16),
            vmem((SD, SLOT), F32),
            vmem((SD, SLOT), BF16),
            vmem((SD, SLOT), F32),
            vmem((2, 512, SLOT), F32),
            vmem((2, 1, SD, SLOT), F32),
            vmem((2, SD, SLOT), BF16),
            vmem((TILES + 1, NB, 2, 16, SLOT), BF16),
            vmem((256, TILES * 2048), BF16),
            vmem((16, 2048), BF16),
            vmem((2, 32, 32, SLOT), BF16),
            vmem((2, 32, 32 * SLOT), BF16),
            vmem((NB, 2, 32, EXTRA), BF16),
            vmem((256, 256), F32),
            vmem((16, 256), F32),
            vmem((16, SUMS, SLOT), F32),
            vmem((16, SUMS, SLOT), F32),
            vmem((SUMS, SLOT), F32),
            vmem((8, SUMS, SLOT), F32),
            vmem((4, SUMS, SLOT), F32),
            sem((10,)),
            sem((NB, TILES)),
            sem((NB, TILES)),
            sem((TILES,)),
            sem((NB,)),
            sem((NB,)),
            sem,
            sem,
            sem,
            sem((GROUPS,)),
            sem,
            sem,
            sem((NB, TILES + 1)),
            sem((NB, TILES + 1)),
            sem,
            sem,
            sem,
            sem,
            sem,
            sem,
            sem,
            pltpu.SemaphoreType.REGULAR,
        ],
        compiler_params=pltpu.CompilerParams(
            collective_id=0, has_side_effects=True, vmem_limit_bytes=62 * 1024 * 1024
        ),
    )(orbitals, trial_bands, potential, stick_column, stick_length, *[jnp.asarray(held[name]) for name in TABLES])
    applied, intersection, projected = pl.pallas_call(
        finish,
        out_shape=(
            jax.ShapeDtypeStruct(trial_bands.shape, F32),
            jax.ShapeDtypeStruct((2, 32, SLOT), F32),
            jax.ShapeDtypeStruct((2, NB, 32), F32),
        ),
        in_specs=[vmem_spec, vmem_spec],
        out_specs=(vmem_spec, vmem_spec, vmem_spec),
    )(applied, final)
    return applied, intersection, jnp.swapaxes(projected, 1, 2)


def solution(mesh):
    return jax.shard_map(
        shards,
        mesh=mesh,
        in_specs=(
            P(None, "band", "plane", None),
            P(None, "band", "plane", None),
            P("plane", None, None),
            P("plane"),
            P("plane"),
        ),
        out_specs=(P(None, "band", "plane", None), P(None, "band", None), P(None, "band", None)),
        check_vma=False,
    )
```
